128 devices in a mesh: dp: 8 (over y_lo, z), ctx: 16 (over x, y_hi, core).
Axes of the slice: x: 4, y: 4 (y_hi: 2, y_lo: 2; y = y_hi * 2 + y_lo), z: 4, core: 2. Of those that a mesh axis runs over, the one named last changes fastest.
Arguments:
- queries: bfloat16 [8, 4096, 2048], P('dp', 'ctx'), may hold values from -30 to 30
- keys: bfloat16 [8, 4096, 128], P('dp', 'ctx'), may hold values from -6 to 6
- values: bfloat16 [8, 4096, 128], P('dp', 'ctx'), may hold values from -6 to 6
- grad_out: bfloat16 [8, 4096, 2048], P('dp', 'ctx'), may hold values from -6 to 6
- assignment: int32 [8, 16, 8], P('dp', 'ctx'), may hold values from 0 to 7, as said below
- doc_lengths: int32 [8, 8], P('dp'), may hold values from 1 to 2048, 4096 in all within a row
Outputs:
- grad_queries: bfloat16 [8, 4096, 2048], P('dp', 'ctx')
- grad_keys: bfloat16 [8, 4096, 128], P('dp', 'ctx')
- grad_values: bfloat16 [8, 4096, 128], P('dp', 'ctx')
The draws below stay inside these ranges and needn't reach their ends.
Inputs may be any that keep to these rules, and one draw needn't show every extreme that they name: For each row r and ctx index c, assignment[r, c, :] is a permutation of 0..7.
All inputs are finite; a program needn't handle non-finite values.
Results may differ from the reference program's by a relative error of at most 0.015.
Values may be sent and summed in bfloat16 or wider, within the bound.
No kernel may reach another device: no remote copies, remote signals or barrier semaphores. Data moves between devices by JAX's collectives and lax.ppermute only.
A program may use at most 128 MiB of HBM per device.

```python
import math
import jax
import jax.numpy as jnp
import numpy as np
from jax import lax

HEADS = 16
HD = 128
TOK_DEV = 256
DOCS = 8
ROWS = 8
SEQ = 4096
MOST = 2048
HQ = 2048
N_DP = 8
N_CTX = 16


def draw_queries(key, part):
    key = jax.random.fold_in(key, 5)
    base = jnp.clip(jax.random.normal(key, (ROWS, SEQ, HEADS * HD), jnp.float32), -6.0, 6.0)
    return base.astype(jnp.bfloat16)


def draw_keys(key, part):
    key = jax.random.fold_in(key, 3)
    base = jnp.clip(jax.random.normal(key, (ROWS, SEQ, HD), jnp.float32), -6.0, 6.0)
    return base.astype(jnp.bfloat16)


def draw_assignment(key, part):
    key = jax.random.fold_in(key, 7)
    many = jax.random.split(key, N_DP * N_CTX)
    perms = jax.vmap(lambda single: jax.random.permutation(single, N_DP))(many)
    return perms.reshape(N_DP, N_CTX, N_DP).astype(jnp.int32)


def levels(rng, shape, shards, low, high):
    level, own = 1.0, jax.random.fold_in(rng, 6)
    for axis_at, parts in shards:
        draws = jnp.exp(jax.random.uniform(jax.random.fold_in(own, axis_at), (parts,), jnp.float32, low / len(shards), high / len(shards)))
        level = level * jnp.repeat(draws, shape[axis_at] // parts).reshape([-1 if axis == axis_at else 1 for axis in range(len(shape))])
    return level


def length_profile(number_of, total, most, skew):
    loads = [(1 << 20) // math.isqrt(grade ** skew) + 1 for grade in range(2, number_of + 1)]
    surplus, given = total - most - (number_of - 1), [1] * (number_of - 1)
    while surplus > 0:
        movable = [i for i in range(number_of - 1) if given[i] < most]
        whole, remaining = sum([loads[i] for i in movable]), surplus
        for i in movable:
            extra = min(most - given[i], max(1, remaining * loads[i] // whole), surplus)
            given[i] = given[i] + extra
            surplus = surplus - extra
    return np.array([most] + given)


def uneven_parts(key, count, total, limit, skew):
    if count == 2:
        one = jax.random.randint(key, (), max(1, total - limit), min(limit, total - 1) + 1)
        return jnp.stack([one, total - one])
    sizes = jnp.asarray(length_profile(count, total, limit, skew), jnp.int32)
    couples = (count - 1) // 2
    giver, receiver = sizes[1:1 + 2 * couples:2], sizes[2:2 + 2 * couples:2]
    slack = jnp.minimum(giver - 1, limit - receiver)
    moved = jax.random.randint(jax.random.fold_in(key, 1), (couples,), 0, 1 << 20) % (slack + 1)
    sizes = sizes.at[1:1 + 2 * couples:2].set(giver - moved).at[2:2 + 2 * couples:2].set(receiver + moved)
    return sizes[jax.random.permutation(jax.random.fold_in(key, 2), count)]


def bell_draw(stream_key, dims, scale, bound, cuts=(), kind=jnp.bfloat16):
    level = levels(stream_key, dims, cuts, -0.22, 0.18) if cuts else 1.0
    values = jax.random.normal(stream_key, dims, jnp.float32) * scale * level
    return jnp.minimum(jnp.maximum(values, -bound), bound).astype(kind)


def setup_inputs(seed: int = 0) -> dict:
    streams_of = jax.random.split(jax.random.key(seed), 7)
    return {
        "queries": draw_queries(jax.random.fold_in(streams_of[6], 71), 0),
        "keys": draw_keys(jax.random.fold_in(streams_of[6], 71), 0),
        "values": bell_draw(streams_of[2], (ROWS, SEQ, HD), 1.0, 6.0, ((0, 8), (1, 16))),
        "grad_out": bell_draw(streams_of[3], (ROWS, SEQ, HQ), 1.0, 6.0, ((0, 8), (1, 16))),
        "assignment": draw_assignment(jax.random.fold_in(streams_of[6], 71), 0),
        "doc_lengths": jax.vmap(lambda own: uneven_parts(own, DOCS, SEQ, MOST, 2))(jax.random.split(streams_of[5], ROWS)).reshape((ROWS, DOCS)).astype(jnp.int32),
    }


def relay(source, assignment):
    width = source.shape[-1]
    piece = TOK_DEV // N_DP
    blocks = source.reshape(N_DP, N_CTX, N_DP, piece, width)
    labels = jnp.arange(N_DP, dtype=jnp.int32)
    onehot = (assignment[:, :, :, None] == labels[None, None, None, :]).astype(jnp.int32)
    inverse = jnp.sum(onehot * labels[None, None, :, None], axis=2).astype(jnp.int32)
    index = jnp.broadcast_to(inverse[:, :, :, None, None], (N_DP, N_CTX, N_DP, piece, width))
    picked = jnp.take_along_axis(blocks, index, axis=2)
    moved = jnp.transpose(picked, (2, 1, 0, 3, 4))
    return moved.reshape(N_DP, SEQ, width)


def segments(lengths):
    ends = jnp.cumsum(lengths).astype(jnp.int32)
    places = jnp.arange(SEQ, dtype=jnp.int32)
    return jnp.sum((places[:, None] >= ends[None, :]).astype(jnp.int32), axis=1)


def one_row(args):
    q_row, k_row, v_row, g_row, lengths = args
    scale = HD ** -0.5
    seg = segments(lengths)
    places = jnp.arange(SEQ, dtype=jnp.int32)
    visible = (seg[:, None] == seg[None, :]) & (places[None, :] <= places[:, None])
    k32 = k_row.astype(jnp.float32)
    v32 = v_row.astype(jnp.float32)
    hp = lax.Precision.HIGHEST

    def head(pair):
        q_head, g_head = pair
        q32 = q_head.astype(jnp.float32)
        g32 = g_head.astype(jnp.float32)
        scores = jnp.dot(q32, k32.T, precision=hp) * scale
        dprob = jnp.dot(g32, v32.T, precision=hp)
        scores = jnp.where(visible, scores, -jnp.inf)
        top = jnp.max(scores, axis=1, keepdims=True)
        expo = jnp.where(visible, jnp.exp(scores - top), 0.0)
        total = jnp.sum(expo, axis=1, keepdims=True)
        lse = top + jnp.log(total)
        delta = jnp.sum(expo * dprob, axis=1, keepdims=True) / total
        prob = jnp.where(visible, jnp.exp(scores - lse), 0.0)
        dscore = prob * (dprob - delta)
        prob16 = prob.astype(jnp.bfloat16).astype(jnp.float32)
        dscore16 = dscore.astype(jnp.bfloat16).astype(jnp.float32)
        grad_v = jnp.dot(prob16.T, g32, precision=hp)
        grad_k = jnp.dot(dscore16.T, q32, precision=hp)
        grad_q = (jnp.dot(dscore16, k32, precision=hp) * scale).astype(jnp.bfloat16)
        return grad_q, grad_k, grad_v

    q_heads = jnp.transpose(q_row.reshape(SEQ, HEADS, HD), (1, 0, 2))
    g_heads = jnp.transpose(g_row.reshape(SEQ, HEADS, HD), (1, 0, 2))
    grad_q, grad_k, grad_v = lax.map(head, (q_heads, g_heads))
    grad_q = jnp.transpose(grad_q, (1, 0, 2)).reshape(SEQ, HEADS * HD)
    grad_k = (scale * jnp.sum(grad_k, axis=0)).astype(jnp.bfloat16)
    grad_v = jnp.sum(grad_v, axis=0).astype(jnp.bfloat16)
    return grad_q, grad_k, grad_v


def reference(queries, keys, values, grad_out, assignment, doc_lengths):
    q_all = relay(queries, assignment)
    k_all = relay(keys, assignment)
    v_all = relay(values, assignment)
    g_all = relay(grad_out, assignment)
    grad_queries, grad_keys, grad_values = lax.map(one_row, (q_all, k_all, v_all, g_all, doc_lengths))
    return grad_queries, grad_keys, grad_values
```

```python
import functools

import jax
import jax.numpy as jnp
from jax import lax
from jax.experimental import pallas as pl
from jax.experimental.pallas import tpu as pltpu
from jax.sharding import PartitionSpec as P

HEADS = 16
HD = 128
ROWS = 8
CHUNK = 256
PIECE = 32
REACH = 9
DOCS = 8
GROUP = 4
SCALE = HD ** (-0.5)
LOG2E = 1.4426950408889634
F32 = jnp.float32
BF16 = jnp.bfloat16


def dot(a, b, dims):
    return lax.dot_general(a, b, (dims, ((), ())), preferred_element_type=F32)


def attention_kernel(group, pieces, scal, *refs):
    sent = refs[:pieces]
    mine, other, dq_ref, even_ref, odd_ref = refs[pieces : pieces + 5]
    win, win_t, qs, gs, s_buf, dp_buf, dqt, dk, dv, stat = refs[pieces + 5 :]
    step = pl.program_id(0)
    me, ctx = scal[0], scal[1]
    width = pieces * PIECE
    cols = group * width
    base = ctx * CHUNK

    end, first_start = jnp.int32(0), jnp.int32(0)
    for i in range(DOCS):
        end = end + scal[2 + i]
        first_start = jnp.where(base >= end, end, first_start)
    count = ctx - lax.shift_right_logical(first_start, 8) + 1

    @pl.when(step == 0)
    def _():
        core = jnp.bitwise_and(ctx, 1)
        for e in range(REACH):
            if e % 2 == 0:
                block = mine[e // 2]
            else:
                block = other[(e - 1) // 2 + 1 - core]
            win[e] = block
            win_t[e] = block[:, :HD].astype(F32).T.astype(BF16)
        dk[...] = jnp.zeros_like(dk)
        dv[...] = jnp.zeros_like(dv)

    for h in range(group):
        for i in range(pieces):
            rows = slice(h * width + i * PIECE, h * width + (i + 1) * PIECE)
            qs[rows, :] = sent[i][0, :, h * HD : (h + 1) * HD]
            gs[rows, :] = sent[i][1, :, h * HD : (h + 1) * HD]

    at = lax.broadcasted_iota(jnp.int32, (1, cols), 1)
    slot = jnp.bitwise_and(lax.shift_right_logical(at, 5), pieces - 1)
    place = base + jnp.bitwise_xor(slot, me) * PIECE + jnp.bitwise_and(at, PIECE - 1)
    start = jnp.zeros((1, cols), jnp.int32)
    end = jnp.int32(0)
    for i in range(DOCS):
        end = end + scal[2 + i]
        start = jnp.where(place >= end, end, start)

    dqt[...] = jnp.zeros_like(dqt)
    row = lax.broadcasted_iota(jnp.int32, (CHUNK, 1), 0)

    def scores(e, carry):
        top, total, accum = carry
        k = win[e, :, :HD]
        v = win[e, :, HD:]
        s = dot(k, qs[...], ((1,), (1,)))
        dp = dot(v, gs[...], ((1,), (1,)))
        key = base - e * CHUNK + row
        seen = (key >= start) & (key <= place)
        s = jnp.where(seen, s * (SCALE * LOG2E), -jnp.inf)
        s_buf[e] = s
        dp_buf[e] = dp
        top_new = jnp.maximum(top, jnp.max(s, axis=0, keepdims=True))
        fade = jnp.exp2(top - top_new)
        p = jnp.exp2(s - top_new)
        total = total * fade + jnp.sum(p, axis=0, keepdims=True)
        accum = accum * fade + jnp.sum(p * dp, axis=0, keepdims=True)
        return top_new, total, accum

    zero = jnp.zeros((1, cols), F32)
    top, total, accum = lax.fori_loop(
        0, count, scores, (jnp.full((1, cols), -jnp.inf, F32), zero, zero)
    )
    stat[0:1, :] = top + jnp.log2(total)
    stat[1:2, :] = accum / total

    def grads(e, carry):
        p = jnp.exp2(s_buf[e] - stat[0:1, :])
        ds = (p * (dp_buf[e] - stat[1:2, :])).astype(BF16)
        dv[e] += dot(p.astype(BF16), gs[...], ((1,), (0,)))
        dk[e] += dot(ds, qs[...], ((1,), (0,)))
        dqt[...] += dot(win_t[e], ds, ((1,), (0,)))
        return carry

    lax.fori_loop(0, count, grads, 0)

    for h in range(group):
        grad = (dqt[:, h * width : (h + 1) * width] * SCALE).T.astype(BF16)
        for i in range(pieces):
            rows = pl.ds(pl.multiple_of(jnp.bitwise_xor(me, i) * PIECE, PIECE), PIECE)
            dq_ref[rows, h * HD : (h + 1) * HD] = grad[i * PIECE : (i + 1) * PIECE]

    @pl.when(step == HEADS // group - 1)
    def _():
        for e in range(REACH):
            if e % 2 == 0:
                even_ref[e // 2, :, :HD] = dk[e] * SCALE
                even_ref[e // 2, :, HD:] = dv[e]
            else:
                odd_ref[e // 2, :, :HD] = (dk[e] * SCALE).astype(BF16)
                odd_ref[e // 2, :, HD:] = dv[e].astype(BF16)


def attention(scal, sent, mine, other, group=GROUP):
    pieces = len(sent)
    cols = group * pieces * PIECE
    whole = lambda shape: pl.BlockSpec(shape, lambda i, s: (0,) * len(shape))
    return pl.pallas_call(
        functools.partial(attention_kernel, group, pieces),
        grid_spec=pltpu.PrefetchScalarGridSpec(
            num_scalar_prefetch=1,
            grid=(HEADS // group,),
            in_specs=[pl.BlockSpec((2, PIECE, group * HD), lambda i, s: (0, 0, i))] * pieces
            + [whole((5, CHUNK, 2 * HD)), whole((5, CHUNK, 2 * HD))],
            out_specs=[
                pl.BlockSpec((CHUNK, group * HD), lambda i, s: (0, i)),
                whole((5, CHUNK, 2 * HD)),
                whole((4, CHUNK, 2 * HD)),
            ],
            scratch_shapes=[
                pltpu.VMEM((REACH, CHUNK, 2 * HD), BF16),
                pltpu.VMEM((REACH, HD, CHUNK), BF16),
                pltpu.VMEM((cols, HD), BF16),
                pltpu.VMEM((cols, HD), BF16),
                pltpu.VMEM((REACH, CHUNK, cols), F32),
                pltpu.VMEM((REACH, CHUNK, cols), F32),
                pltpu.VMEM((HD, cols), F32),
                pltpu.VMEM((REACH, CHUNK, HD), F32),
                pltpu.VMEM((REACH, CHUNK, HD), F32),
                pltpu.VMEM((8, cols), F32),
            ],
        ),
        out_shape=[
            jax.ShapeDtypeStruct((CHUNK, HEADS * HD), BF16),
            jax.ShapeDtypeStruct((5, CHUNK, 2 * HD), F32),
            jax.ShapeDtypeStruct((4, CHUNK, 2 * HD), BF16),
        ],
        compiler_params=pltpu.CompilerParams(vmem_limit_bytes=56 * 2**20),
        cost_estimate=pl.CostEstimate(
            flops=20_000_000_000, bytes_accessed=8 * 2**20, transcendentals=0
        ),
    )(scal, *sent, mine, other)


def on_device(queries, keys, values, grad_out, assignment, doc_lengths):
    me = lax.axis_index("dp")
    ctx = lax.axis_index("ctx")
    assign_row = assignment[0, 0]
    labels = jnp.arange(ROWS, dtype=jnp.int32)
    onehot = (assign_row[:, None] == labels[None, :]).astype(jnp.int32)
    inverse = jnp.sum(onehot * labels[:, None], axis=0)
    scal = jnp.concatenate([jnp.stack([me, ctx]).astype(jnp.int32), doc_lengths[0]])

    kv = jnp.concatenate([keys[0], values[0]], axis=1).reshape(ROWS, PIECE, 2 * HD)
    kv = lax.all_to_all(
        jnp.take(kv, inverse, axis=0), "dp", split_axis=0, concat_axis=0, tiled=True
    ).reshape(CHUNK, 2 * HD)

    qg = jnp.stack(
        [queries[0].reshape(ROWS, PIECE, HEADS * HD), grad_out[0].reshape(ROWS, PIECE, HEADS * HD)],
        axis=1,
    )
    sent = []
    for d in range(ROWS):
        piece = lax.dynamic_index_in_dim(qg, inverse[me ^ d], 0, keepdims=False)
        if d:
            piece = lax.ppermute(piece, "dp", [(i, i ^ d) for i in range(ROWS)])
        sent.append(piece)

    back = [lax.ppermute(kv, "ctx", [(i, i + 2 * s) for i in range(16 - 2 * s)]) for s in range(1, 5)]
    mine = jnp.stack([kv] + back)
    swap = [(i, i ^ 1) for i in range(16)]
    other = lax.ppermute(mine, "ctx", swap)

    grad_q, even, odd = attention(scal, sent, mine, other)

    core = jnp.bitwise_and(ctx, 1)
    got = lax.ppermute(odd, "ctx", swap)
    padded = jnp.pad(got, ((1, 1), (0, 0), (0, 0)))
    shares = even + lax.dynamic_slice_in_dim(padded, 1 - core, 5, 0).astype(F32)
    total = shares[0]
    for s in range(1, 5):
        share = shares[s].astype(BF16)
        share = lax.ppermute(share, "ctx", [(i, i - 2 * s) for i in range(2 * s, 16)])
        total = total + share.astype(F32)
    grad_kv = total.astype(BF16)
    return grad_q[None], grad_kv[None, :, :HD], grad_kv[None, :, HD:]


def solution(mesh):
    in_specs = (
        P("dp", "ctx", None),
        P("dp", "ctx", None),
        P("dp", "ctx", None),
        P("dp", "ctx", None),
        P("dp", "ctx", None),
        P("dp", None),
    )
    out_specs = (P("dp", "ctx", None), P("dp", "ctx", None), P("dp", "ctx", None))
    return jax.shard_map(
        on_device, mesh=mesh, in_specs=in_specs, out_specs=out_specs, check_vma=False
    )
```

```python
import functools

import jax
import jax.numpy as jnp
from jax import lax
from jax.experimental import pallas as pl
from jax.experimental.pallas import tpu as pltpu
from jax.sharding import PartitionSpec as P

HEADS = 16
HD = 128
ROWS = 8
CTX = 16
CHUNK = 256
PIECE = 32
REACH = 9
SPAN = 3
DOCS = 8
GROUP = 4
SCALE = HD ** (-0.5)
LOG2E = 1.4426950408889634
F32 = jnp.float32
BF16 = jnp.bfloat16


def dot(a, b, dims):
    return lax.dot_general(a, b, (dims, ((), ())), preferred_element_type=F32)


def pack_kernel(assign, q, k, v, g, qg_out, kv_out, sems):
    copies = []
    for d in range(ROWS):
        piece = jnp.int32(0)
        for p in range(ROWS):
            piece = jnp.where(assign[0, 0, p] == d, p, piece)
        rows = pl.ds(pl.multiple_of(piece * PIECE, PIECE), PIECE)
        pairs = [
            (k.at[0, rows], kv_out.at[d, :, pl.ds(0, HD)]),
            (v.at[0, rows], kv_out.at[d, :, pl.ds(HD, HD)]),
            (q.at[0, rows], qg_out.at[d, 0]),
            (g.at[0, rows], qg_out.at[d, 1]),
        ]
        for i, (src, dst) in enumerate(pairs):
            copies.append(pltpu.make_async_copy(src, dst, sems.at[d, i]))
    for copy in copies:
        copy.start()
    for copy in copies:
        copy.wait()


def pack(assignment, queries, keys, values, grad_out):
    far = pl.BlockSpec(memory_space=pltpu.HBM)
    near = pl.BlockSpec(memory_space=pltpu.VMEM)
    return pl.pallas_call(
        pack_kernel,
        in_specs=[pl.BlockSpec(memory_space=pltpu.SMEM), far, far, far, far],
        out_specs=[near, near],
        out_shape=[
            jax.ShapeDtypeStruct((ROWS, 2, PIECE, HEADS * HD), BF16),
            jax.ShapeDtypeStruct((ROWS, PIECE, 2 * HD), BF16),
        ],
        scratch_shapes=[pltpu.SemaphoreType.DMA((ROWS, 4))],
        compiler_params=pltpu.CompilerParams(vmem_limit_bytes=60 * 2**20),
    )(assignment, queries, keys, values, grad_out)


def attention_kernel(group, scal, qg, mine, other, dq_ref, even_ref, odd_ref, win, win_t, *rest):
    qs,gs,s_buf,dp_buf,stat=[rest[2*i:2*i+2] for i in range(5)]
    dqt, dk, dv = rest[10:]
    step = pl.program_id(0)
    steps = HEADS//group
    ctx = lax.axis_index("ctx")
    cols = group*CHUNK
    base = ctx*CHUNK
    SB = SPAN
    KB = SB*CHUNK
    end, first_start = jnp.int32(0), jnp.int32(0)
    for i in range(DOCS):
        end = end + scal[0, i]
        first_start = jnp.where(base >= end, end, first_start)
    count = ctx - lax.shift_right_logical(first_start, 8) + 1
    nsb = (count + SB - 1)//SB

    @pl.when(step == 0)
    def _():
        core = jnp.bitwise_and(ctx, 1)
        for e in range(REACH):
            block = mine[e//2] if e%2==0 else other[(e-1)//2+1-core]
            win[e*CHUNK:(e+1)*CHUNK] = block
            win_t[:, e*CHUNK:(e+1)*CHUNK] = block[:, :HD].T
        dk[...] = jnp.zeros_like(dk)
        dv[...] = jnp.zeros_like(dv)

    place = base + jnp.bitwise_and(lax.broadcasted_iota(jnp.int32,(1,cols),1),CHUNK-1)
    start = jnp.zeros((1,cols),jnp.int32)
    end = jnp.int32(0)
    for i in range(DOCS):
        end = end + scal[0, i]
        start = jnp.where(place >= end, end, start)
    row = lax.broadcasted_iota(jnp.int32,(CHUNK,1),0)

    def scores(now, was, sb, first):
        r0 = sb*KB if first else pl.multiple_of(sb*KB, KB)
        s = dot(win[pl.ds(r0,KB),:HD], qs[now][...], ((1,),(1,)))
        dp = dot(win[pl.ds(r0,KB),HD:], gs[now][...], ((1,),(1,)))
        parts=[]
        for u in range(SB):
            key = base - (sb*SB+u)*CHUNK + row
            seen = key >= start
            if first and u==0: seen = seen & (key <= place)
            parts.append(jnp.where(seen, s[u*CHUNK:(u+1)*CHUNK]*(SCALE*LOG2E), -jnp.inf))
        s = jnp.concatenate(parts,0) if SB>1 else parts[0]
        s_buf[now][pl.ds(r0,KB),:] = s
        dp_buf[now][pl.ds(r0,KB),:] = dp
        if first:
            top = jnp.max(s,axis=0,keepdims=True)
            p = jnp.exp2(s - top)
            stat[now][0:1,:] = top
            stat[now][1:2,:] = jnp.sum(p,axis=0,keepdims=True)
            stat[now][2:3,:] = jnp.sum(p*dp,axis=0,keepdims=True)
        else:
            old = stat[now][0:1,:]
            top = jnp.maximum(old, jnp.max(s,axis=0,keepdims=True))
            fade = jnp.exp2(old - top)
            p = jnp.exp2(s - top)
            stat[now][0:1,:] = top
            stat[now][1:2,:] = stat[now][1:2,:]*fade + jnp.sum(p,axis=0,keepdims=True)
            stat[now][2:3,:] = stat[now][2:3,:]*fade + jnp.sum(p*dp,axis=0,keepdims=True)

    def grads(now, was, sb, first):
        r0 = sb*KB if first else pl.multiple_of(sb*KB, KB)
        p = jnp.exp2(s_buf[was][pl.ds(r0,KB),:] - stat[was][0:1,:])
        ds = (p*(dp_buf[was][pl.ds(r0,KB),:] - stat[was][1:2,:])).astype(BF16)
        p = p.astype(BF16)
        dv[pl.ds(r0,KB),:] += dot(p, gs[was][...], ((1,),(0,)))
        dk[pl.ds(r0,KB),:] += dot(ds, qs[was][...], ((1,),(0,)))
        if first: dqt[...] = dot(win_t[:,pl.ds(r0,KB)], ds, ((1,),(0,)))
        else: dqt[...] += dot(win_t[:,pl.ds(r0,KB)], ds, ((1,),(0,)))

    def run(now, fs):
        was = 1-now
        if scores in fs:
            for h in range(group):
                for r in range(ROWS):
                    rows = slice(h*CHUNK + r*PIECE, h*CHUNK + (r+1)*PIECE)
                    qs[now][rows,:] = qg[r,0,:,h*HD:(h+1)*HD]
                    gs[now][rows,:] = qg[r,1,:,h*HD:(h+1)*HD]
        for f in fs: f(now, was, 0, True)
        def body(sb,c):
            for f in fs: f(now, was, sb, False)
            return c
        lax.fori_loop(1,nsb,body,0)
        if scores in fs:
            total = stat[now][1:2,:]
            stat[now][0:1,:] = stat[now][0:1,:] + jnp.log2(total)
            stat[now][1:2,:] = stat[now][2:3,:]/total
    both = [grads,scores]
    @pl.when(step == 0)
    def _(): run(0,[scores])
    @pl.when((step < steps) & (jnp.bitwise_and(step,1)==1))
    def _(): run(1,both)
    if steps>2:
        @pl.when((step > 0) & (step < steps) & (jnp.bitwise_and(step,1)==0))
        def _(): run(0,both)
    @pl.when(step == steps)
    def _(): run(steps%2,[grads])
    @pl.when(step > 0)
    def _():
        for h in range(group):
            dq_ref[:, h*HD:(h+1)*HD] = (dqt[:, h*CHUNK:(h+1)*CHUNK]*SCALE).T.astype(BF16)
    @pl.when(step == steps)
    def _():
        for e in range(REACH):
            rs=slice(e*CHUNK,(e+1)*CHUNK)
            if e%2==0:
                even_ref[e//2,:,:HD] = dk[rs]*SCALE
                even_ref[e//2,:,HD:] = dv[rs]
            else:
                odd_ref[e//2,:,:HD] = (dk[rs]*SCALE).astype(BF16)
                odd_ref[e//2,:,HD:] = dv[rs].astype(BF16)

def attention(scal, qg, mine, other, group=GROUP):
    cols = group*CHUNK
    steps=HEADS//group
    whole = lambda shape: pl.BlockSpec(shape, lambda i, s: (0,)*len(shape))
    return pl.pallas_call(
        functools.partial(attention_kernel, group),
        grid_spec=pltpu.PrefetchScalarGridSpec(
            num_scalar_prefetch=1, grid=(steps+1,),
            in_specs=[pl.BlockSpec((ROWS,2,PIECE,group*HD), lambda i,s:(0,0,0,jnp.minimum(i,steps-1))), whole((5,CHUNK,2*HD)), whole((5,CHUNK,2*HD))],
            out_specs=[pl.BlockSpec((CHUNK,group*HD), lambda i,s:(0,jnp.maximum(i-1,0))), whole((5,CHUNK,2*HD)), whole((4,CHUNK,2*HD))],
            scratch_shapes=[
                pltpu.VMEM((REACH*CHUNK,2*HD),BF16), pltpu.VMEM((HD,REACH*CHUNK),BF16),
                ]+[pltpu.VMEM((cols,HD),BF16)]*4+[pltpu.VMEM((REACH*CHUNK,cols),F32)]*4+[pltpu.VMEM((8,cols),F32)]*2+[
                pltpu.VMEM((HD,cols),F32),
                pltpu.VMEM((REACH*CHUNK,HD),F32), pltpu.VMEM((REACH*CHUNK,HD),F32)]),
        out_shape=[jax.ShapeDtypeStruct((CHUNK,HEADS*HD),BF16), jax.ShapeDtypeStruct((5,CHUNK,2*HD),F32), jax.ShapeDtypeStruct((4,CHUNK,2*HD),BF16)],
        compiler_params=pltpu.CompilerParams(vmem_limit_bytes=60*2**20),
    )(scal, qg, mine, other)


def on_device(queries, keys, values, grad_out, assignment, doc_lengths):
    ctx = lax.axis_index("ctx")
    qg, kv = pack(assignment, queries, keys, values, grad_out)
    kv = lax.all_to_all(kv, "dp", split_axis=0, concat_axis=0, tiled=True)
    kv = kv.reshape(CHUNK, 2 * HD)
    qg = lax.all_to_all(qg, "dp", split_axis=0, concat_axis=0, tiled=True)

    swap = [(i, i ^ 1) for i in range(CTX)]
    back = [
        lax.ppermute(kv, "ctx", [(i, i + 2 * s) for i in range(CTX - 2 * s)]) for s in range(1, 5)
    ]
    mine = jnp.stack([kv] + back)
    other = lax.ppermute(mine, "ctx", swap)

    grad_q, even, odd = attention(doc_lengths, qg, mine, other)

    core = jnp.bitwise_and(ctx, 1)
    got = lax.ppermute(odd, "ctx", swap)
    padded = jnp.pad(got, ((1, 1), (0, 0), (0, 0)))
    shares = even + lax.dynamic_slice_in_dim(padded, 1 - core, 5, 0).astype(F32)
    total = shares[0]
    for s in range(1, 5):
        share = shares[s].astype(BF16)
        share = lax.ppermute(share, "ctx", [(i, i - 2 * s) for i in range(2 * s, CTX)])
        total = total + share.astype(F32)
    grad_kv = total.astype(BF16)
    return grad_q[None], grad_kv[None, :, :HD], grad_kv[None, :, HD:]


def solution(mesh):
    in_specs = (
        P("dp", "ctx", None),
        P("dp", "ctx", None),
        P("dp", "ctx", None),
        P("dp", "ctx", None),
        P("dp", "ctx", None),
        P("dp", None),
    )
    out_specs = (P("dp", "ctx", None), P("dp", "ctx", None), P("dp", "ctx", None))
    return jax.shard_map(
        on_device, mesh=mesh, in_specs=in_specs, out_specs=out_specs, check_vma=False
    )
```

```python
import functools

import jax
import jax.numpy as jnp
from jax import lax
from jax.experimental import pallas as pl
from jax.experimental.pallas import tpu as pltpu
from jax.sharding import PartitionSpec as P

HEADS = 16
HD = 128
ROWS = 8
CTX = 16
CHUNK = 256
PIECE = 32
REACH = 9
SPAN = 3
DOCS = 8
GROUP = 4
FIRST = 4
SCALE = HD ** (-0.5)
LOG2E = 1.4426950408889634
F32 = jnp.float32
BF16 = jnp.bfloat16


def dot(a, b, dims):
    return lax.dot_general(a, b, (dims, ((), ())), preferred_element_type=F32)


def pack_kernel(assign, q, k, v, g, first, rest, sems):
    wide = FIRST * HD
    copies = []
    for d in range(ROWS):
        piece = jnp.int32(0)
        for p in range(ROWS):
            piece = jnp.where(assign[0, 0, p] == d, p, piece)
        rows = pl.ds(pl.multiple_of(piece * PIECE, PIECE), PIECE)
        near, far = pl.ds(0, wide), pl.ds(wide, HEADS * HD - wide)
        pairs = [
            (k.at[0, rows], first.at[d, 0, :, pl.ds(wide, HD)]),
            (v.at[0, rows], first.at[d, 1, :, pl.ds(wide, HD)]),
            (q.at[0, rows, near], first.at[d, 0, :, near]),
            (g.at[0, rows, near], first.at[d, 1, :, near]),
            (q.at[0, rows, far], rest.at[d, 0]),
            (g.at[0, rows, far], rest.at[d, 1]),
        ]
        for i, (src, dst) in enumerate(pairs):
            copies.append(pltpu.make_async_copy(src, dst, sems.at[d, i]))
    for copy in copies:
        copy.start()
    for copy in copies:
        copy.wait()


def pack(assignment, queries, keys, values, grad_out):
    far = pl.BlockSpec(memory_space=pltpu.HBM)
    near = pl.BlockSpec(memory_space=pltpu.VMEM)
    return pl.pallas_call(
        pack_kernel,
        in_specs=[pl.BlockSpec(memory_space=pltpu.SMEM), far, far, far, far],
        out_specs=[near, near],
        out_shape=[
            jax.ShapeDtypeStruct((ROWS, 2, PIECE, (FIRST + 1) * HD), BF16),
            jax.ShapeDtypeStruct((ROWS, 2, PIECE, (HEADS - FIRST) * HD), BF16),
        ],
        scratch_shapes=[pltpu.SemaphoreType.DMA((ROWS, 6))],
        compiler_params=pltpu.CompilerParams(vmem_limit_bytes=60 * 2**20),
    )(assignment, queries, keys, values, grad_out)


def attention_kernel(group, scal, qg_first, qg_rest, mine, other, dq_ref, even_ref, odd_ref, win, win_t, *rest):
    qs,gs,s_buf,dp_buf,stat=[rest[2*i:2*i+2] for i in range(5)]
    dqt, dk, dv = rest[10:]
    step = pl.program_id(0)
    steps = HEADS//group
    ctx = lax.axis_index("ctx")
    cols = group*CHUNK
    base = ctx*CHUNK
    SB = SPAN
    KB = SB*CHUNK
    end, first_start = jnp.int32(0), jnp.int32(0)
    for i in range(DOCS):
        end = end + scal[0, i]
        first_start = jnp.where(base >= end, end, first_start)
    count = ctx - lax.shift_right_logical(first_start, 8) + 1
    nsb = (count + SB - 1)//SB

    @pl.when(step == 0)
    def _():
        core = jnp.bitwise_and(ctx, 1)
        for e in range(REACH):
            block = mine[e//2] if e%2==0 else other[(e-1)//2+1-core]
            win[e*CHUNK:(e+1)*CHUNK] = block
            win_t[:, e*CHUNK:(e+1)*CHUNK] = block[:, :HD].T
        dk[...] = jnp.zeros_like(dk)
        dv[...] = jnp.zeros_like(dv)

    place = base + jnp.bitwise_and(lax.broadcasted_iota(jnp.int32,(1,cols),1),CHUNK-1)
    start = jnp.zeros((1,cols),jnp.int32)
    end = jnp.int32(0)
    for i in range(DOCS):
        end = end + scal[0, i]
        start = jnp.where(place >= end, end, start)
    row = lax.broadcasted_iota(jnp.int32,(CHUNK,1),0)

    def scores(now, was, sb, first):
        r0 = sb*KB if first else pl.multiple_of(sb*KB, KB)
        s = dot(win[pl.ds(r0,KB),:HD], qs[now][...], ((1,),(1,)))
        dp = dot(win[pl.ds(r0,KB),HD:], gs[now][...], ((1,),(1,)))
        parts=[]
        for u in range(SB):
            key = base - (sb*SB+u)*CHUNK + row
            seen = key >= start
            if first and u==0: seen = seen & (key <= place)
            parts.append(jnp.where(seen, s[u*CHUNK:(u+1)*CHUNK]*(SCALE*LOG2E), -jnp.inf))
        s = jnp.concatenate(parts,0) if SB>1 else parts[0]
        s_buf[now][pl.ds(r0,KB),:] = s
        dp_buf[now][pl.ds(r0,KB),:] = dp
        if first:
            top = jnp.max(s,axis=0,keepdims=True)
            p = jnp.exp2(s - top)
            stat[now][0:1,:] = top
            stat[now][1:2,:] = jnp.sum(p,axis=0,keepdims=True)
            stat[now][2:3,:] = jnp.sum(p*dp,axis=0,keepdims=True)
        else:
            old = stat[now][0:1,:]
            top = jnp.maximum(old, jnp.max(s,axis=0,keepdims=True))
            fade = jnp.exp2(old - top)
            p = jnp.exp2(s - top)
            stat[now][0:1,:] = top
            stat[now][1:2,:] = stat[now][1:2,:]*fade + jnp.sum(p,axis=0,keepdims=True)
            stat[now][2:3,:] = stat[now][2:3,:]*fade + jnp.sum(p*dp,axis=0,keepdims=True)

    def grads(now, was, sb, first):
        r0 = sb*KB if first else pl.multiple_of(sb*KB, KB)
        p = jnp.exp2(s_buf[was][pl.ds(r0,KB),:] - stat[was][0:1,:])
        ds = (p*(dp_buf[was][pl.ds(r0,KB),:] - stat[was][1:2,:])).astype(BF16)
        p = p.astype(BF16)
        dv[pl.ds(r0,KB),:] += dot(p, gs[was][...], ((1,),(0,)))
        dk[pl.ds(r0,KB),:] += dot(ds, qs[was][...], ((1,),(0,)))
        if first: dqt[...] = dot(win_t[:,pl.ds(r0,KB)], ds, ((1,),(0,)))
        else: dqt[...] += dot(win_t[:,pl.ds(r0,KB)], ds, ((1,),(0,)))

    def run(now, fs):
        was = 1-now
        if scores in fs:
            qg = qg_first if grads not in fs else qg_rest
            for h in range(group):
                for r in range(ROWS):
                    rows = slice(h*CHUNK + r*PIECE, h*CHUNK + (r+1)*PIECE)
                    qs[now][rows,:] = qg[r,0,:,h*HD:(h+1)*HD]
                    gs[now][rows,:] = qg[r,1,:,h*HD:(h+1)*HD]
        for f in fs: f(now, was, 0, True)
        def body(sb,c):
            for f in fs: f(now, was, sb, False)
            return c
        lax.fori_loop(1,nsb,body,0)
        if scores in fs:
            total = stat[now][1:2,:]
            stat[now][0:1,:] = stat[now][0:1,:] + jnp.log2(total)
            stat[now][1:2,:] = stat[now][2:3,:]/total
    both = [grads,scores]
    @pl.when(step == 0)
    def _(): run(0,[scores])
    @pl.when((step < steps) & (jnp.bitwise_and(step,1)==1))
    def _(): run(1,both)
    if steps>2:
        @pl.when((step > 0) & (step < steps) & (jnp.bitwise_and(step,1)==0))
        def _(): run(0,both)
    @pl.when(step == steps)
    def _(): run(steps%2,[grads])
    @pl.when(step > 0)
    def _():
        for h in range(group):
            dq_ref[:, h*HD:(h+1)*HD] = (dqt[:, h*CHUNK:(h+1)*CHUNK]*SCALE).T.astype(BF16)
    @pl.when(step == steps)
    def _():
        for e in range(REACH):
            rs=slice(e*CHUNK,(e+1)*CHUNK)
            if e%2==0:
                even_ref[e//2,:,:HD] = dk[rs]*SCALE
                even_ref[e//2,:,HD:] = dv[rs]
            else:
                odd_ref[e//2,:,:HD] = (dk[rs]*SCALE).astype(BF16)
                odd_ref[e//2,:,HD:] = dv[rs].astype(BF16)

def attention(scal, qg_first, qg_rest, mine, other, group=GROUP):
    cols = group*CHUNK
    steps=HEADS//group
    whole = lambda shape: pl.BlockSpec(shape, lambda i, s: (0,)*len(shape))
    return pl.pallas_call(
        functools.partial(attention_kernel, group),
        grid_spec=pltpu.PrefetchScalarGridSpec(
            num_scalar_prefetch=1, grid=(steps+1,),
            in_specs=[
                pl.BlockSpec((ROWS,2,PIECE,group*HD), lambda i,s:(0,0,0,0)),
                pl.BlockSpec((ROWS,2,PIECE,group*HD), lambda i,s:(0,0,0,jnp.clip(i-1,0,steps-2))), whole((5,CHUNK,2*HD)), whole((5,CHUNK,2*HD))],
            out_specs=[pl.BlockSpec((CHUNK,group*HD), lambda i,s:(0,jnp.maximum(i-1,0))), whole((5,CHUNK,2*HD)), whole((4,CHUNK,2*HD))],
            scratch_shapes=[
                pltpu.VMEM((REACH*CHUNK,2*HD),BF16), pltpu.VMEM((HD,REACH*CHUNK),BF16),
                ]+[pltpu.VMEM((cols,HD),BF16)]*4+[pltpu.VMEM((REACH*CHUNK,cols),F32)]*4+[pltpu.VMEM((8,cols),F32)]*2+[
                pltpu.VMEM((HD,cols),F32),
                pltpu.VMEM((REACH*CHUNK,HD),F32), pltpu.VMEM((REACH*CHUNK,HD),F32)]),
        out_shape=[jax.ShapeDtypeStruct((CHUNK,HEADS*HD),BF16), jax.ShapeDtypeStruct((5,CHUNK,2*HD),F32), jax.ShapeDtypeStruct((4,CHUNK,2*HD),BF16)],
        compiler_params=pltpu.CompilerParams(vmem_limit_bytes=58*2**20),
    )(scal, qg_first, qg_rest, mine, other)


def on_device(queries, keys, values, grad_out, assignment, doc_lengths):
    ctx = lax.axis_index("ctx")
    first, rest = pack(assignment, queries, keys, values, grad_out)
    first = lax.all_to_all(first, "dp", split_axis=0, concat_axis=0, tiled=True)
    rest = lax.all_to_all(rest, "dp", split_axis=0, concat_axis=0, tiled=True)
    kv = first[:, :, :, FIRST * HD :]
    kv = jnp.concatenate([kv[:, 0], kv[:, 1]], axis=-1).reshape(CHUNK, 2 * HD)

    swap = [(i, i ^ 1) for i in range(CTX)]
    back = [
        lax.ppermute(kv, "ctx", [(i, i + 2 * s) for i in range(CTX - 2 * s)]) for s in range(1, 5)
    ]
    mine = jnp.stack([kv] + back)
    other = lax.ppermute(mine, "ctx", swap)

    grad_q, even, odd = attention(doc_lengths, first, rest, mine, other)

    core = jnp.bitwise_and(ctx, 1)
    got = lax.ppermute(odd, "ctx", swap)
    padded = jnp.pad(got, ((1, 1), (0, 0), (0, 0)))
    shares = even + lax.dynamic_slice_in_dim(padded, 1 - core, 5, 0).astype(F32)
    total = shares[0]
    for s in range(1, 5):
        share = shares[s].astype(BF16)
        share = lax.ppermute(share, "ctx", [(i, i - 2 * s) for i in range(2 * s, CTX)])
        total = total + share.astype(F32)
    grad_kv = total.astype(BF16)
    return grad_q[None], grad_kv[None, :, :HD], grad_kv[None, :, HD:]


def solution(mesh):
    in_specs = (
        P("dp", "ctx", None),
        P("dp", "ctx", None),
        P("dp", "ctx", None),
        P("dp", "ctx", None),
        P("dp", "ctx", None),
        P("dp", None),
    )
    out_specs = (P("dp", "ctx", None), P("dp", "ctx", None), P("dp", "ctx", None))
    return jax.shard_map(
        on_device, mesh=mesh, in_specs=in_specs, out_specs=out_specs, check_vma=False
    )
```

```python
import functools

import jax
import jax.numpy as jnp
from jax import lax
from jax.experimental import pallas as pl
from jax.experimental.pallas import tpu as pltpu
from jax.sharding import PartitionSpec as P

HEADS = 16
HD = 128
ROWS = 8
CTX = 16
CHUNK = 256
PIECE = 32
REACH = 9
SPAN = 3
DOCS = 8
GROUP = 4
FIRST = 4
SCALE = HD ** (-0.5)
LOG2E = 1.4426950408889634
F32 = jnp.float32
BF16 = jnp.bfloat16


def dot(a, b, dims):
    return lax.dot_general(a, b, (dims, ((), ())), preferred_element_type=F32)


def pack_kernel(assign, q, k, v, g, first, rest, first_buf, rest_buf, sems, out_sems):
    wide = FIRST * HD
    near, far = pl.ds(0, wide), pl.ds(wide, HEADS * HD - wide)
    reads, writes = [], []
    for d in range(ROWS):
        piece = jnp.int32(0)
        for p in range(ROWS):
            piece = jnp.where(assign[0, 0, p] == d, p, piece)
        rows = pl.ds(pl.multiple_of(piece * PIECE, PIECE), PIECE)
        pairs = [
            (k.at[0, rows], first_buf.at[d, 0, :, pl.ds(wide, HD)]),
            (v.at[0, rows], first_buf.at[d, 1, :, pl.ds(wide, HD)]),
            (q.at[0, rows, near], first_buf.at[d, 0, :, near]),
            (g.at[0, rows, near], first_buf.at[d, 1, :, near]),
            (q.at[0, rows, far], rest_buf.at[d, 0]),
            (g.at[0, rows, far], rest_buf.at[d, 1]),
        ]
        reads.append(
            [pltpu.make_async_copy(src, dst, sems.at[d, i]) for i, (src, dst) in enumerate(pairs)]
        )
        writes.append(
            [
                pltpu.make_async_copy(first_buf.at[d], first.at[d], out_sems.at[d, 0]),
                pltpu.make_async_copy(rest_buf.at[d], rest.at[d], out_sems.at[d, 1]),
            ]
        )
        for copy in reads[d]:
            copy.start()
    for d in range(ROWS):
        for copy in reads[d]:
            copy.wait()
        for copy in writes[d]:
            copy.start()
    for copies in writes:
        for copy in copies:
            copy.wait()


def pack(assignment, queries, keys, values, grad_out):
    far = pl.BlockSpec(memory_space=pltpu.HBM)
    shapes = [
        (ROWS, 2, PIECE, (FIRST + 1) * HD),
        (ROWS, 2, PIECE, (HEADS - FIRST) * HD),
    ]
    return pl.pallas_call(
        pack_kernel,
        in_specs=[pl.BlockSpec(memory_space=pltpu.SMEM), far, far, far, far],
        out_specs=[far, far],
        out_shape=[jax.ShapeDtypeStruct(shape, BF16) for shape in shapes],
        scratch_shapes=[
            pltpu.VMEM(shapes[0], BF16),
            pltpu.VMEM(shapes[1], BF16),
            pltpu.SemaphoreType.DMA((ROWS, 6)),
            pltpu.SemaphoreType.DMA((ROWS, 2)),
        ],
        compiler_params=pltpu.CompilerParams(vmem_limit_bytes=60 * 2**20),
    )(assignment, queries, keys, values, grad_out)


def window_kernel(mine, other, rest, win, win_t):
    core = jnp.bitwise_and(lax.axis_index("ctx"), 1)
    for e in range(REACH):
        block = mine[e // 2] if e % 2 == 0 else other[(e - 1) // 2 + 1 - core]
        rows = slice(e * CHUNK, (e + 1) * CHUNK)
        win[rows] = block
        win_t[:, rows] = block[:, :HD].T


def window(mine, other, rest):
    near = pl.BlockSpec(memory_space=pltpu.VMEM)
    return pl.pallas_call(
        window_kernel,
        in_specs=[near, near, pl.BlockSpec(memory_space=pl.ANY)],
        out_specs=[near, near],
        out_shape=[
            jax.ShapeDtypeStruct((REACH * CHUNK, 2 * HD), BF16),
            jax.ShapeDtypeStruct((HD, REACH * CHUNK), BF16),
        ],
        compiler_params=pltpu.CompilerParams(vmem_limit_bytes=16 * 2**20),
    )(mine, other, rest)


def attention_kernel(group, scal, qg_first, qg_rest, win, win_t, dq_ref, even_ref, odd_ref, *rest):
    qs, gs, stat = [rest[2 * i : 2 * i + 2] for i in range(3)]
    s_buf, dp_buf = rest[6:7] * 2, rest[7:8] * 2
    dqt, dk, dv = rest[8:]
    step = pl.program_id(0)
    steps = HEADS//group
    ctx = lax.axis_index("ctx")
    cols = group*CHUNK
    base = ctx*CHUNK
    SB = SPAN
    KB = SB*CHUNK
    end, first_start = jnp.int32(0), jnp.int32(0)
    for i in range(DOCS):
        end = end + scal[0, i]
        first_start = jnp.where(base >= end, end, first_start)
    count = ctx - lax.shift_right_logical(first_start, 8) + 1
    nsb = (count + SB - 1)//SB

    @pl.when(step == 0)
    def _():
        dk[...] = jnp.zeros_like(dk)
        dv[...] = jnp.zeros_like(dv)

    place = base + jnp.bitwise_and(lax.broadcasted_iota(jnp.int32,(1,cols),1),CHUNK-1)
    start = jnp.zeros((1,cols),jnp.int32)
    end = jnp.int32(0)
    for i in range(DOCS):
        end = end + scal[0, i]
        start = jnp.where(place >= end, end, start)
    row = lax.broadcasted_iota(jnp.int32,(CHUNK,1),0)

    def scores(now, was, sb, first):
        r0 = sb*KB
        s = dot(win[pl.ds(r0,KB),:HD], qs[now][...], ((1,),(1,)))
        dp = dot(win[pl.ds(r0,KB),HD:], gs[now][...], ((1,),(1,)))
        parts=[]
        for u in range(SB):
            key = base - (sb*SB+u)*CHUNK + row
            seen = key >= start
            if first and u==0: seen = seen & (key <= place)
            parts.append(jnp.where(seen, s[u*CHUNK:(u+1)*CHUNK]*(SCALE*LOG2E), -jnp.inf))
        s = jnp.concatenate(parts,0) if SB>1 else parts[0]
        s_buf[now][pl.ds(r0,KB),:] = s
        dp_buf[now][pl.ds(r0,KB),:] = dp
        if first:
            top = jnp.max(s,axis=0,keepdims=True)
            p = jnp.exp2(s - top)
            stat[now][0:1,:] = top
            stat[now][1:2,:] = jnp.sum(p,axis=0,keepdims=True)
            stat[now][2:3,:] = jnp.sum(p*dp,axis=0,keepdims=True)
        else:
            old = stat[now][0:1,:]
            top = jnp.maximum(old, jnp.max(s,axis=0,keepdims=True))
            fade = jnp.exp2(old - top)
            p = jnp.exp2(s - top)
            stat[now][0:1,:] = top
            stat[now][1:2,:] = stat[now][1:2,:]*fade + jnp.sum(p,axis=0,keepdims=True)
            stat[now][2:3,:] = stat[now][2:3,:]*fade + jnp.sum(p*dp,axis=0,keepdims=True)

    def grads(now, was, sb, first):
        r0 = sb*KB
        p = jnp.exp2(s_buf[was][pl.ds(r0,KB),:] - stat[was][0:1,:])
        ds = (p*(dp_buf[was][pl.ds(r0,KB),:] - stat[was][1:2,:])).astype(BF16)
        p = p.astype(BF16)
        dv[pl.ds(r0,KB),:] += dot(p, gs[was][...], ((1,),(0,)))
        dk[pl.ds(r0,KB),:] += dot(ds, qs[was][...], ((1,),(0,)))
        if first: dqt[...] = dot(win_t[:,pl.ds(r0,KB)], ds, ((1,),(0,)))
        else: dqt[...] += dot(win_t[:,pl.ds(r0,KB)], ds, ((1,),(0,)))

    def run(now, fs):
        was = 1-now
        if scores in fs:
            qg = qg_first if grads not in fs else qg_rest
            for h in range(group):
                for r in range(ROWS):
                    rows = slice(h*CHUNK + r*PIECE, h*CHUNK + (r+1)*PIECE)
                    qs[now][rows,:] = qg[r,0,:,h*HD:(h+1)*HD]
                    gs[now][rows,:] = qg[r,1,:,h*HD:(h+1)*HD]
        for f in fs: f(now, was, 0, True)
        @pl.when(nsb == 3)
        def _():
            for sb in (1, 2):
                for f in fs: f(now, was, sb, False)
        @pl.when(nsb == 2)
        def _():
            for f in fs: f(now, was, 1, False)
        if scores in fs:
            total = stat[now][1:2,:]
            stat[now][0:1,:] = stat[now][0:1,:] + jnp.log2(total)
            stat[now][1:2,:] = stat[now][2:3,:]/total
    both = [grads, scores]
    @pl.when(step == 0)
    def _(): run(0,[scores])
    @pl.when((step < steps) & (jnp.bitwise_and(step,1)==1))
    def _(): run(1,both)
    if steps>2:
        @pl.when((step > 0) & (step < steps) & (jnp.bitwise_and(step,1)==0))
        def _(): run(0,both)
    @pl.when(step == steps)
    def _(): run(steps%2,[grads])
    @pl.when(step > 0)
    def _():
        for h in range(group):
            dq_ref[:, h*HD:(h+1)*HD] = (dqt[:, h*CHUNK:(h+1)*CHUNK]*SCALE).astype(BF16).T
    @pl.when(step == steps)
    def _():
        for e in range(REACH):
            rs=slice(e*CHUNK,(e+1)*CHUNK)
            if e%2==0:
                even_ref[e//2,:,:HD] = dk[rs]*SCALE
                even_ref[e//2,:,HD:] = dv[rs]
            else:
                odd_ref[e//2,:,:HD] = (dk[rs]*SCALE).astype(BF16)
                odd_ref[e//2,:,HD:] = dv[rs].astype(BF16)

def attention(scal, qg_first, qg_rest, win, win_t, group=GROUP):
    cols = group*CHUNK
    steps=HEADS//group
    near = pl.BlockSpec(memory_space=pltpu.VMEM)
    return pl.pallas_call(
        functools.partial(attention_kernel, group),
        grid_spec=pltpu.PrefetchScalarGridSpec(
            num_scalar_prefetch=1, grid=(steps+1,),
            in_specs=[
                near,
                pl.BlockSpec((ROWS,2,PIECE,group*HD), lambda i,s:(0,0,0,jnp.clip(i-1,0,steps-2))), near, near],
            out_specs=[pl.BlockSpec((CHUNK,group*HD), lambda i,s:(0,jnp.maximum(i-1,0))), near, near],
            scratch_shapes=[
                ]+[pltpu.VMEM((cols,HD),BF16)]*4+[pltpu.VMEM((8,cols),F32)]*2+[pltpu.VMEM((REACH*CHUNK,cols),F32)]*2+[
                pltpu.VMEM((HD,cols),F32),
                pltpu.VMEM((REACH*CHUNK,HD),F32), pltpu.VMEM((REACH*CHUNK,HD),F32)]),
        out_shape=[jax.ShapeDtypeStruct((CHUNK,HEADS*HD),BF16), jax.ShapeDtypeStruct((5,CHUNK,2*HD),F32), jax.ShapeDtypeStruct((4,CHUNK,2*HD),BF16)],
        compiler_params=pltpu.CompilerParams(vmem_limit_bytes=40*2**20),
    )(scal, qg_first, qg_rest, win, win_t)


def on_device(queries, keys, values, grad_out, assignment, doc_lengths):
    ctx = lax.axis_index("ctx")
    first, rest = pack(assignment, queries, keys, values, grad_out)
    first = lax.all_to_all(first, "dp", split_axis=0, concat_axis=0, tiled=True)
    rest = lax.all_to_all(rest, "dp", split_axis=0, concat_axis=0, tiled=True)
    kv = first[:, :, :, FIRST * HD :]
    kv = jnp.concatenate([kv[:, 0], kv[:, 1]], axis=-1).reshape(CHUNK, 2 * HD)

    swap = [(i, i ^ 1) for i in range(CTX)]
    back = [
        lax.ppermute(kv, "ctx", [(i, i + 2 * s) for i in range(CTX - 2 * s)]) for s in range(1, 5)
    ]
    mine = jnp.stack([kv] + back)
    other = lax.ppermute(mine, "ctx", swap)

    win, win_t = window(mine, other, rest)
    grad_q, even, odd = attention(doc_lengths, first, rest, win, win_t)

    core = jnp.bitwise_and(ctx, 1)
    got = lax.ppermute(odd, "ctx", swap)
    padded = jnp.pad(got, ((1, 1), (0, 0), (0, 0)))
    shares = even + lax.dynamic_slice_in_dim(padded, 1 - core, 5, 0).astype(F32)
    total = shares[0]
    for s in range(1, 5):
        share = shares[s].astype(BF16)
        share = lax.ppermute(share, "ctx", [(i, i - 2 * s) for i in range(2 * s, CTX)])
        total = total + share.astype(F32)
    grad_kv = total.astype(BF16)
    return grad_q[None], grad_kv[None, :, :HD], grad_kv[None, :, HD:]


def solution(mesh):
    in_specs = (
        P("dp", "ctx", None),
        P("dp", "ctx", None),
        P("dp", "ctx", None),
        P("dp", "ctx", None),
        P("dp", "ctx", None),
        P("dp", None),
    )
    out_specs = (P("dp", "ctx", None), P("dp", "ctx", None), P("dp", "ctx", None))
    return jax.shard_map(
        on_device, mesh=mesh, in_specs=in_specs, out_specs=out_specs, check_vma=False
    )
```

```python
import functools

import jax
import jax.numpy as jnp
from jax import lax
from jax.experimental import pallas as pl
from jax.experimental.pallas import tpu as pltpu
from jax.sharding import PartitionSpec as P

HEADS = 16
HD = 128
ROWS = 8
CTX = 16
CHUNK = 256
PIECE = 32
REACH = 9
SPAN = 3
DOCS = 8
GROUP = 4
FIRST = 4
SCALE = HD ** (-0.5)
LOG2E = 1.4426950408889634
F32 = jnp.float32
BF16 = jnp.bfloat16


def dot(a, b, dims):
    return lax.dot_general(a, b, (dims, ((), ())), preferred_element_type=F32)


def pack_kernel(assign, q, k, v, g, first, rest, first_buf, rest_buf, sems, out_sems):
    wide = FIRST * HD
    near, far = pl.ds(0, wide), pl.ds(wide, HEADS * HD - wide)
    reads, writes = [], []
    for d in range(ROWS):
        piece = jnp.int32(0)
        for p in range(ROWS):
            piece = jnp.where(assign[0, 0, p] == d, p, piece)
        rows = pl.ds(pl.multiple_of(piece * PIECE, PIECE), PIECE)
        pairs = [
            (k.at[0, rows], first_buf.at[d, 0, :, pl.ds(wide, HD)]),
            (v.at[0, rows], first_buf.at[d, 1, :, pl.ds(wide, HD)]),
            (q.at[0, rows, near], first_buf.at[d, 0, :, near]),
            (g.at[0, rows, near], first_buf.at[d, 1, :, near]),
            (q.at[0, rows, far], rest_buf.at[d, 0]),
            (g.at[0, rows, far], rest_buf.at[d, 1]),
        ]
        reads.append(
            [pltpu.make_async_copy(src, dst, sems.at[d, i]) for i, (src, dst) in enumerate(pairs)]
        )
        writes.append(
            [
                pltpu.make_async_copy(first_buf.at[d], first.at[d], out_sems.at[d, 0]),
                pltpu.make_async_copy(rest_buf.at[d], rest.at[d], out_sems.at[d, 1]),
            ]
        )
        for copy in reads[d]:
            copy.start()
    for d in range(ROWS):
        for copy in reads[d]:
            copy.wait()
        for copy in writes[d]:
            copy.start()
    for copies in writes:
        for copy in copies:
            copy.wait()


def pack(assignment, queries, keys, values, grad_out):
    far = pl.BlockSpec(memory_space=pltpu.HBM)
    shapes = [
        (ROWS, 2, PIECE, (FIRST + 1) * HD),
        (ROWS, 2, PIECE, (HEADS - FIRST) * HD),
    ]
    return pl.pallas_call(
        pack_kernel,
        in_specs=[pl.BlockSpec(memory_space=pltpu.SMEM), far, far, far, far],
        out_specs=[far, far],
        out_shape=[jax.ShapeDtypeStruct(shape, BF16) for shape in shapes],
        scratch_shapes=[
            pltpu.VMEM(shapes[0], BF16),
            pltpu.VMEM(shapes[1], BF16),
            pltpu.SemaphoreType.DMA((ROWS, 6)),
            pltpu.SemaphoreType.DMA((ROWS, 2)),
        ],
        compiler_params=pltpu.CompilerParams(vmem_limit_bytes=60 * 2**20),
    )(assignment, queries, keys, values, grad_out)


def window_kernel(mine, other, rest, win, win_t):
    core = jnp.bitwise_and(lax.axis_index("ctx"), 1)
    for e in range(REACH):
        block = mine[e // 2] if e % 2 == 0 else other[(e - 1) // 2 + 1 - core]
        rows = slice(e * CHUNK, (e + 1) * CHUNK)
        win[rows] = block
        win_t[:, rows] = block[:, :HD].T


def window(mine, other, rest):
    near = pl.BlockSpec(memory_space=pltpu.VMEM)
    return pl.pallas_call(
        window_kernel,
        in_specs=[near, near, pl.BlockSpec(memory_space=pl.ANY)],
        out_specs=[near, near],
        out_shape=[
            jax.ShapeDtypeStruct((REACH * CHUNK, 2 * HD), BF16),
            jax.ShapeDtypeStruct((HD, REACH * CHUNK), BF16),
        ],
        compiler_params=pltpu.CompilerParams(vmem_limit_bytes=16 * 2**20),
    )(mine, other, rest)


def attention_kernel(group, scal, qg_first, qg_rest, win, win_t, dq_ref, even_ref, odd_ref, *rest):
    qs, gs, stat = [rest[2 * i : 2 * i + 2] for i in range(3)]
    s_buf, dp_buf = rest[6:7] * 2, rest[7:8] * 2
    dqt, dk, dv = rest[8:]
    step = pl.program_id(0)
    steps = HEADS//group
    ctx = lax.axis_index("ctx")
    cols = group*CHUNK
    base = ctx*CHUNK
    SB = SPAN
    KB = SB*CHUNK
    end, first_start = jnp.int32(0), jnp.int32(0)
    for i in range(DOCS):
        end = end + scal[0, i]
        first_start = jnp.where(base >= end, end, first_start)
    count = ctx - lax.shift_right_logical(first_start, 8) + 1
    nsb = (count + SB - 1)//SB

    @pl.when(step == 0)
    def _():
        dk[...] = jnp.zeros_like(dk)
        dv[...] = jnp.zeros_like(dv)

    place = base + jnp.bitwise_and(lax.broadcasted_iota(jnp.int32,(1,cols),1),CHUNK-1)
    start = jnp.zeros((1,cols),jnp.int32)
    end = jnp.int32(0)
    for i in range(DOCS):
        end = end + scal[0, i]
        start = jnp.where(place >= end, end, start)
    row = lax.broadcasted_iota(jnp.int32,(CHUNK,1),0)

    def scores(now, was, sb, first):
        r0 = sb*KB
        s = dot(win[pl.ds(r0,KB),:HD], qs[now][...], ((1,),(1,)))
        dp = dot(win[pl.ds(r0,KB),HD:], gs[now][...], ((1,),(1,)))
        parts=[]
        for u in range(SB):
            key = base - (sb*SB+u)*CHUNK + row
            seen = key >= start
            if first and u==0: seen = seen & (key <= place)
            parts.append(jnp.where(seen, s[u*CHUNK:(u+1)*CHUNK]*(SCALE*LOG2E), -jnp.inf))
        s = jnp.concatenate(parts,0) if SB>1 else parts[0]
        s_buf[now][pl.ds(r0,KB),:] = s
        dp_buf[now][pl.ds(r0,KB),:] = dp
        if first:
            top = jnp.max(s,axis=0,keepdims=True)
            p = jnp.exp2(s - top)
            stat[now][0:1,:] = top
            stat[now][1:2,:] = jnp.sum(p,axis=0,keepdims=True)
            stat[now][2:3,:] = jnp.sum(p*dp,axis=0,keepdims=True)
        else:
            old = stat[now][0:1,:]
            top = jnp.maximum(old, jnp.max(s,axis=0,keepdims=True))
            fade = jnp.exp2(old - top)
            p = jnp.exp2(s - top)
            stat[now][0:1,:] = top
            stat[now][1:2,:] = stat[now][1:2,:]*fade + jnp.sum(p,axis=0,keepdims=True)
            stat[now][2:3,:] = stat[now][2:3,:]*fade + jnp.sum(p*dp,axis=0,keepdims=True)

    def grads(now, was, sb, first):
        r0 = sb*KB
        p = jnp.exp2(s_buf[was][pl.ds(r0,KB),:] - stat[was][0:1,:])
        ds = (p*(dp_buf[was][pl.ds(r0,KB),:] - stat[was][1:2,:])).astype(BF16)
        p = p.astype(BF16)
        dv[pl.ds(r0,KB),:] += dot(p, gs[was][...], ((1,),(0,)))
        dk[pl.ds(r0,KB),:] += dot(ds, qs[was][...], ((1,),(0,)))
        if first: dqt[...] = dot(win_t[:,pl.ds(r0,KB)], ds, ((1,),(0,)))
        else: dqt[...] += dot(win_t[:,pl.ds(r0,KB)], ds, ((1,),(0,)))

    def run(now, fs):
        was = 1-now
        if scores in fs:
            qg = qg_first if grads not in fs else qg_rest
            for h in range(group):
                for r in range(ROWS):
                    rows = slice(h*CHUNK + r*PIECE, h*CHUNK + (r+1)*PIECE)
                    qs[now][rows,:] = qg[r,0,:,h*HD:(h+1)*HD]
                    gs[now][rows,:] = qg[r,1,:,h*HD:(h+1)*HD]
        for f in fs: f(now, was, 0, True)
        @pl.when(nsb == 3)
        def _():
            for sb in (1, 2):
                for f in fs: f(now, was, sb, False)
        @pl.when(nsb == 2)
        def _():
            for f in fs: f(now, was, 1, False)
        if scores in fs:
            total = stat[now][1:2,:]
            stat[now][0:1,:] = stat[now][0:1,:] + jnp.log2(total)
            stat[now][1:2,:] = stat[now][2:3,:]/total
    both = [grads, scores]
    @pl.when(step == 0)
    def _(): run(0,[scores])
    @pl.when((step < steps) & (jnp.bitwise_and(step,1)==1))
    def _(): run(1,both)
    if steps>2:
        @pl.when((step > 0) & (step < steps) & (jnp.bitwise_and(step,1)==0))
        def _(): run(0,both)
    @pl.when(step == steps)
    def _(): run(steps%2,[grads])
    @pl.when(step > 0)
    def _():
        for h in range(group):
            dq_ref[:, h*HD:(h+1)*HD] = (dqt[:, h*CHUNK:(h+1)*CHUNK]*SCALE).astype(BF16).T
    @pl.when(step == steps)
    def _():
        for e in range(REACH):
            rs=slice(e*CHUNK,(e+1)*CHUNK)
            if e%2==0:
                even_ref[e//2,:,:HD] = dk[rs]*SCALE
                even_ref[e//2,:,HD:] = dv[rs]
            else:
                odd_ref[e//2,:,:HD] = (dk[rs]*SCALE).astype(BF16)
                odd_ref[e//2,:,HD:] = dv[rs].astype(BF16)

def attention(scal, qg_first, qg_rest, win, win_t, group=GROUP):
    cols = group*CHUNK
    steps=HEADS//group
    near = pl.BlockSpec(memory_space=pltpu.VMEM)
    return pl.pallas_call(
        functools.partial(attention_kernel, group),
        grid_spec=pltpu.PrefetchScalarGridSpec(
            num_scalar_prefetch=1, grid=(steps+1,),
            in_specs=[
                near,
                pl.BlockSpec((ROWS,2,PIECE,group*HD), lambda i,s:(0,0,0,jnp.clip(i-1,0,steps-2))), near, near],
            out_specs=[pl.BlockSpec((CHUNK,group*HD), lambda i,s:(0,jnp.maximum(i-1,0))), near, near],
            scratch_shapes=[
                ]+[pltpu.VMEM((cols,HD),BF16)]*4+[pltpu.VMEM((8,cols),F32)]*2+[pltpu.VMEM((REACH*CHUNK,cols),F32)]*2+[
                pltpu.VMEM((HD,cols),F32),
                pltpu.VMEM((REACH*CHUNK,HD),F32), pltpu.VMEM((REACH*CHUNK,HD),F32)]),
        out_shape=[jax.ShapeDtypeStruct((CHUNK,HEADS*HD),BF16), jax.ShapeDtypeStruct((5,CHUNK,2*HD),F32), jax.ShapeDtypeStruct((4,CHUNK,2*HD),BF16)],
        compiler_params=pltpu.CompilerParams(vmem_limit_bytes=40*2**20),
    )(scal, qg_first, qg_rest, win, win_t)


def on_device(queries, keys, values, grad_out, assignment, doc_lengths):
    ctx = lax.axis_index("ctx")
    first, rest = pack(assignment, queries, keys, values, grad_out)
    first = lax.all_to_all(first, "dp", split_axis=0, concat_axis=0, tiled=True)
    rest = lax.all_to_all(rest, "dp", split_axis=0, concat_axis=0, tiled=True)
    kv = first[:, :, :, FIRST * HD :]
    kv = jnp.concatenate([kv[:, 0], kv[:, 1]], axis=-1).reshape(CHUNK, 2 * HD)

    swap = [(i, i ^ 1) for i in range(CTX)]
    back = [
        lax.ppermute(kv, "ctx", [(i, i + 2 * s) for i in range(CTX - 2 * s)]) for s in range(4, 0, -1)
    ]
    mine = jnp.stack([kv] + back[::-1])
    other = lax.ppermute(mine, "ctx", swap)

    win, win_t = window(mine, other, rest)
    grad_q, even, odd = attention(doc_lengths, first, rest, win, win_t)

    core = jnp.bitwise_and(ctx, 1)
    got = lax.ppermute(odd, "ctx", swap)
    padded = jnp.pad(got, ((1, 1), (0, 0), (0, 0)))
    shares = even + lax.dynamic_slice_in_dim(padded, 1 - core, 5, 0).astype(F32)
    total = shares[0]
    for s in range(4, 0, -1):
        share = shares[s].astype(BF16)
        share = lax.ppermute(share, "ctx", [(i, i - 2 * s) for i in range(2 * s, CTX)])
        total = total + share.astype(F32)
    grad_kv = total.astype(BF16)
    return grad_q[None], grad_kv[None, :, :HD], grad_kv[None, :, HD:]


def solution(mesh):
    in_specs = (
        P("dp", "ctx", None),
        P("dp", "ctx", None),
        P("dp", "ctx", None),
        P("dp", "ctx", None),
        P("dp", "ctx", None),
        P("dp", None),
    )
    out_specs = (P("dp", "ctx", None), P("dp", "ctx", None), P("dp", "ctx", None))
    return jax.shard_map(
        on_device, mesh=mesh, in_specs=in_specs, out_specs=out_specs, check_vma=False
    )
```
